256 devices in a mesh: tm: 32 (over z_hi, x, core), chan: 4 (over y), bank: 2 (over z_lo).
Axes of the slice: x: 4, y: 4, z: 8 (z_hi: 4, z_lo: 2; z = z_hi * 2 + z_lo), core: 2. Of those that a mesh axis runs over, the one named last changes fastest.
Arguments:
- record: bfloat16 [512, 131072], P('chan', ('tm', 'bank')), as said below
- templates: bfloat16 [2048, 512, 256], P(('tm', 'bank'), 'chan'), as said below
- block_ids: int32 [2], replicated, may hold values from 0 to 63
- sensor_group: int32 [512], P('chan'), may hold values from 0 to 3
Outputs:
- traces: float32 [2, 32, 131072], P(None, 'chan', ('tm', 'bank'))
The draws below stay inside these ranges and needn't reach their ends.
Inputs may be any that keep to these rules, and one draw needn't show every extreme that they name: `record`: real-valued samples of order one to a few tens, scales differing from sensor to sensor. `templates`: real-valued template samples.
All inputs are finite; a program needn't handle non-finite values.
Results may differ from the reference program's by a relative error of at most 0.0003.
Values may be sent and summed in bfloat16 or wider, within the bound.
No kernel may reach another device: no remote copies, remote signals or barrier semaphores. Data moves between devices by JAX's collectives and lax.ppermute only.
A program may use at most 64 MiB of HBM per device.

```python
import math
import jax
import jax.numpy as jnp
from jax import lax

SENSORS = 512
K = 32
TLEN = 256
GROUPS = 4
DSTEP = 64
ROUNDS = 2
SAMPLES = 131072
NBLOCKS = 64
HALO = 512


def sensor_scale(key, sensor_count, spread):
    position = jnp.arange(sensor_count, dtype=jnp.float32)
    jitter = jnp.exp(jax.random.uniform(key, (sensor_count,), jnp.float32) * math.log(spread))
    return jnp.exp(math.log(3.0) * position / max(sensor_count - 1, 1)) * jitter


def draw_record(key, part):
    key = jax.random.fold_in(key, 11)
    gain_key, value_key = jax.random.split(key)
    gains = sensor_scale(gain_key, SENSORS, 4.0)
    values = jnp.clip(jax.random.normal(value_key, (SENSORS, SAMPLES), jnp.float32), -6.0, 6.0)
    return (values * gains[:, None]).astype(jnp.bfloat16)


def draw_templates(key, part):
    key = jax.random.fold_in(key, 23)
    gain_key, value_key = jax.random.split(key, 2)
    gains = sensor_scale(gain_key, SENSORS, 4.0)
    shape = (NBLOCKS * K, SENSORS, TLEN)
    values = jnp.clip(jax.random.normal(value_key, shape, jnp.float32), -6.0, 6.0)
    return (values * gains[None, :, None]).astype(jnp.bfloat16)


def place_ends(drawn, rng, smallest, top_value):
    extent = drawn.shape
    place = [jax.random.randint(jax.random.fold_in(rng, axis), (), 0, extent[axis]) for axis in range(len(extent))]
    drawn = drawn.at[tuple(place)].set(smallest)
    longest = extent.index(max(extent))
    place[longest] = (place[longest] + 1) % extent[longest]
    return drawn.at[tuple(place)].set(top_value)


def setup_inputs(seed: int = 0) -> dict:
    key_list = jax.random.split(jax.random.key(seed), 5)
    return {
        "record": draw_record(jax.random.fold_in(key_list[4], 71), 0),
        "templates": draw_templates(jax.random.fold_in(key_list[4], 71), 0),
        "block_ids": jax.random.randint(key_list[2], (ROUNDS,), 0, NBLOCKS).astype(jnp.int32),
        "sensor_group": place_ends(jax.random.randint(key_list[3], (SENSORS,), 0, GROUPS), jax.random.fold_in(key_list[3], 1), 0, GROUPS - 1).astype(jnp.int32),
    }


def reference(record, templates, block_ids, sensor_group):
    ext_width = SAMPLES + TLEN
    padded = jnp.pad(record, ((0, 0), (0, HALO)))
    delayed = jnp.zeros((SENSORS, ext_width), jnp.bfloat16)
    for group_id in range(GROUPS):
        moved = padded[:, DSTEP * group_id:DSTEP * group_id + ext_width]
        delayed = jnp.where((sensor_group == group_id)[:, None], moved, delayed)
    widened = delayed.astype(jnp.float32)
    chosen = templates.reshape(NBLOCKS, K, SENSORS, TLEN)[block_ids]
    weights = chosen.astype(jnp.float32).reshape(ROUNDS * K, SENSORS, TLEN)
    tmpl_norm = lax.optimization_barrier(jnp.sum(weights * weights, axis=(1, 2))).reshape(ROUNDS, K)
    power_sum = lax.optimization_barrier(jnp.sum(widened * widened, axis=0))

    def add_tap(carry, tap_index):
        correlation, energy = carry
        window = lax.dynamic_slice_in_dim(widened, tap_index, SAMPLES, 1)
        tap_weights = lax.dynamic_index_in_dim(weights, tap_index, 2, keepdims=False)
        correlation = correlation + jnp.dot(tap_weights, window, precision=lax.Precision.HIGHEST, preferred_element_type=jnp.float32)
        energy = energy + lax.dynamic_slice_in_dim(power_sum, tap_index, SAMPLES, 0)
        return ((correlation, energy), None)
    start_carry = (jnp.zeros((ROUNDS * K, SAMPLES), jnp.float32), jnp.zeros((SAMPLES,), jnp.float32))
    (correlation, energy), _ = lax.scan(add_tap, start_carry, jnp.arange(TLEN, dtype=jnp.int32))
    correlation = correlation.reshape(ROUNDS, K, SAMPLES)
    unit_scale = math.sqrt(SENSORS * TLEN)
    return correlation * unit_scale / jnp.sqrt(tmpl_norm[:, :, None] * (energy[None, None, :] + 1e-05))
```

```python
import math

import jax
import jax.numpy as jnp
from jax import lax
from jax.experimental import pallas as pl
from jax.experimental.pallas import tpu as pltpu
from jax.sharding import Mesh, PartitionSpec as P

SENSORS = 512
TLEN = 256
GROUPS = 4
DSTEP = 64
HALO = 512
TILE = 2048
EXT = TILE + TLEN
FINE = 8
COARSE = TLEN // FINE
NX, NZ, NY = 4, 8, 4
SUB = 16
DEPTH = FINE * NY * SUB
ROWS = 2 * COARSE
HALF = NX * ROWS
TIME_TILE = 768
VMEM_LIMIT = 40 * 1024 * 1024

PLANE = ("zh", "x", "bank")
ZAXES = ("zh", "bank")
BLOCKS = ("zh", "x", "core", "bank")


def shift(value, axis, steps):
    count = lax.axis_size(axis)
    return lax.ppermute(value, axis, [(i, (i + steps) % count) for i in range(count)])


def plane_index(x, z):
    return ((z // 2) * NX + x) * 2 + z % 2


def turn_kernel(*refs):
    inputs, out_ref, turned_ref = refs[:NY], refs[NY], refs[NY + 1]
    rows = [ref[r].astype(jnp.float32) for r in range(2) for ref in inputs]
    turned_ref[...] = jnp.concatenate(rows, 0).T
    for pair in range(FINE // 2):
        even = turned_ref[pl.ds(2 * pair, COARSE, stride=FINE), :].astype(jnp.bfloat16)
        odd = turned_ref[pl.ds(2 * pair + 1, COARSE, stride=FINE), :].astype(jnp.bfloat16)
        for r in range(2):
            lanes = slice(64 * r, 64 * r + 64)
            out_ref[COARSE * r : COARSE * (r + 1), 128 * pair : 128 * (pair + 1)] = jnp.concatenate(
                [even[:, lanes], odd[:, lanes]], 1
            )


def turn(parts):
    return pl.pallas_call(
        turn_kernel,
        out_shape=jax.ShapeDtypeStruct((ROWS, DEPTH), jnp.bfloat16),
        scratch_shapes=[pltpu.VMEM((TLEN, 128), jnp.float32)],
        name="turn",
    )(*parts)


def join_kernel(x_ref, *refs):
    inputs, out_ref, wide_ref = refs[:NX], refs[NX], refs[NX + 1]
    for d, ref in enumerate(inputs):
        kk = lax.rem(x_ref[0] + NX - d, NX)
        for r in range(2):
            block = ref[COARSE * r : COARSE * (r + 1), :].astype(jnp.float32)
            for i in range(DEPTH // 128):
                rows = pl.ds(NX * r + kk, COARSE, stride=2 * NX)
                wide_ref[i, rows, :] = block[:, 128 * i : 128 * (i + 1)]
    for i in range(DEPTH // 128):
        out_ref[:, 128 * i : 128 * (i + 1)] = wide_ref[i].astype(jnp.bfloat16)


def join(x, parts):
    return pl.pallas_call(
        join_kernel,
        grid_spec=pltpu.PrefetchScalarGridSpec(
            num_scalar_prefetch=1,
            grid=(1,),
            in_specs=[pl.BlockSpec((ROWS, DEPTH), lambda n, i: (0, 0))] * NX,
            out_specs=pl.BlockSpec((HALF, DEPTH), lambda n, i: (0, 0)),
            scratch_shapes=[pltpu.VMEM((DEPTH // 128, HALF, 128), jnp.float32)],
        ),
        out_shape=jax.ShapeDtypeStruct((HALF, DEPTH), jnp.bfloat16),
        name="join",
    )(x[None], *parts)


def spread_kernel(*refs):
    inputs, x2_ref, energy_ref, power_ref = refs[:NY], refs[NY], refs[NY + 1], refs[NY + 2]
    step = pl.program_id(0)

    @pl.when(step == 0)
    def _():
        power_ref[...] = jnp.zeros_like(power_ref)

    rows = jnp.concatenate([ref[...].astype(jnp.float32) for ref in inputs], 0)
    power_ref[...] += jnp.sum((rows * rows).reshape(NY * SUB // 8, 8, EXT), 0)
    for e in range(FINE):
        moved = pltpu.roll(rows, EXT - e, 1) if e else rows
        x2_ref[0, 64 * e : 64 * (e + 1), :] = moved.astype(jnp.bfloat16)

    @pl.when(step == pl.num_programs(0) - 1)
    def _():
        total = power_ref[...]
        width = 1
        while width < TLEN:
            total = total + pltpu.roll(total, EXT - width, 1)
            width *= 2
        energy_ref[...] = jnp.sum(total, 0, keepdims=True)[:, :TILE]


def spread(sensors):
    return pl.pallas_call(
        spread_kernel,
        grid=(NZ,),
        in_specs=[pl.BlockSpec((SUB, EXT), lambda n: (n, 0))] * NY,
        out_specs=[
            pl.BlockSpec((1, DEPTH, EXT), lambda n: (n, 0, 0)),
            pl.BlockSpec((1, TILE), lambda n: (0, 0)),
        ],
        out_shape=[
            jax.ShapeDtypeStruct((NZ, DEPTH, EXT), jnp.bfloat16),
            jax.ShapeDtypeStruct((1, TILE), jnp.float32),
        ],
        scratch_shapes=[pltpu.VMEM((8, EXT), jnp.float32)],
        compiler_params=pltpu.CompilerParams(vmem_limit_bytes=VMEM_LIMIT),
        cost_estimate=pl.CostEstimate(flops=2**24, bytes_accessed=24 * 2**20, transcendentals=0),
        name="spread",
    )(*sensors)


def square_sums(left):
    wide = left.astype(jnp.float32)
    wide = wide * wide
    total = wide[:, :128]
    for i in range(128, wide.shape[1], 128):
        total = total + wide[:, i : i + 128]
    return total


def fold(y_ref, start):
    split = COARSE // 2
    parts = []
    for j in range(split):
        near, far = start + 8 * j, start + 8 * (j + split)
        parts.append(y_ref[near : near + 8, : EXT - 128] + y_ref[far : far + 8, 128:])
    width = FINE
    while len(parts) > 1:
        parts = [
            parts[i] + pltpu.roll(parts[i + 1], EXT - 128 - width, 1)
            for i in range(0, len(parts), 2)
        ]
        width *= 2
    return parts[0][:, :TILE]


def correlate_kernel(blocks, places, seeded, closing, index_ref, *refs):
    refs = list(refs)
    take = lambda n: [refs.pop(0) for _ in range(n)]
    lefts = [take(n) for n in blocks]
    x2_ref = take(1)[0]
    extra_refs = take(2 * seeded + closing)
    outs = take(1 if closing else 2)
    y_ref, left_ref, right_ref = take(3)
    extras = take(len(extra_refs))
    sem_ref = take(1)[0]
    used = 0

    def begin(source, target):
        nonlocal used
        copy = pltpu.make_async_copy(source, target, sem_ref.at[used])
        copy.start()
        used += 1
        return copy

    left_copies = []
    for c, group in enumerate(lefts):
        row = 0
        for ref in group:
            target = left_ref.at[row : row + ref.shape[0], DEPTH * c : DEPTH * (c + 1)]
            left_copies.append(begin(ref, target))
            row += ref.shape[0]
    right_copies = []
    for t in range(EXT // TIME_TILE):
        lanes = slice(TIME_TILE * t, TIME_TILE * (t + 1))
        right_copies.append(
            [
                begin(
                    x2_ref.at[index_ref[place], :, lanes],
                    right_ref.at[t, DEPTH * c : DEPTH * (c + 1)],
                )
                for c, place in enumerate(places)
            ]
        )
    extra_copies = [begin(ref, extra) for ref, extra in zip(extra_refs, extras)]
    for copy in left_copies:
        copy.wait()
    for t in range(EXT // TIME_TILE):
        for copy in right_copies[t]:
            copy.wait()
        y_ref[:, TIME_TILE * t : TIME_TILE * (t + 1)] = jnp.dot(
            left_ref[...], right_ref[t], preferred_element_type=jnp.float32
        )
    for copy in extra_copies:
        copy.wait()

    norm = square_sums(left_ref[...])
    sums = [fold(y_ref, half * HALF) for half in range(2)]
    if seeded:
        norm = norm + extras[1][...]
        sums = [sums[half] + extras[0][8 * half : 8 * half + 8] for half in range(2)]
    if not closing:
        for half in range(2):
            outs[0][8 * half : 8 * half + 8, :] = sums[half]
        outs[1][...] = norm
        return
    scale = math.sqrt(SENSORS * TLEN)
    level = extras[2][...] + 1e-05
    for half in range(2):
        squares = jnp.sum(norm[half * HALF : (half + 1) * HALF].reshape(COARSE, 8, 128), 0)
        squares = jnp.sum(squares, 1, keepdims=True)
        sums[half] = sums[half] * scale * lax.rsqrt(squares * level)
    first = index_ref[NZ] == 0
    low = jnp.where(first, sums[0], sums[1])
    high = jnp.where(first, sums[1], sums[0])
    for r in range(2):
        outs[0][r, :NX, :] = low[NX * r : NX * (r + 1)]
        outs[0][r, NX:, :] = high[NX * r : NX * (r + 1)]


def correlate(index, places, lefts, x2, before=None, energy=None):
    count = len(lefts)
    seeded, closing = before is not None, energy is not None
    extra = (list(before) if seeded else []) + ([energy] if closing else [])
    operands = [ref for group in lefts for ref in group] + [x2] + extra
    if closing:
        out_shape = jax.ShapeDtypeStruct((2, 8, TILE), jnp.float32)
    else:
        out_shape = [
            jax.ShapeDtypeStruct((16, TILE), jnp.float32),
            jax.ShapeDtypeStruct((2 * HALF, 128), jnp.float32),
        ]
    blocks = [len(group) for group in lefts]
    tiles = EXT // TIME_TILE
    return pl.pallas_call(
        lambda *refs: correlate_kernel(blocks, list(places), seeded, closing, *refs),
        in_specs=[pl.BlockSpec(memory_space=pltpu.SMEM)]
        + [pl.BlockSpec(memory_space=pl.ANY)] * len(operands),
        scratch_shapes=[
            pltpu.VMEM((2 * HALF, EXT), jnp.float32),
            pltpu.VMEM((2 * HALF, DEPTH * count), jnp.bfloat16),
            pltpu.VMEM((tiles, DEPTH * count, TIME_TILE), jnp.bfloat16),
            *[pltpu.VMEM(a.shape, a.dtype) for a in extra],
            pltpu.SemaphoreType.DMA((sum(blocks) + tiles * count + len(extra),)),
        ],
        out_shape=out_shape,
        compiler_params=pltpu.CompilerParams(vmem_limit_bytes=VMEM_LIMIT),
        cost_estimate=pl.CostEstimate(
            flops=2 * 2 * HALF * DEPTH * count * EXT,
            bytes_accessed=count * 3 * 2**20,
            transcendentals=0,
        ),
        name="correlate",
    )(index, *operands)


def local(record, templates, block_ids, sensor_group):
    zh, x, core = lax.axis_index("zh"), lax.axis_index("x"), lax.axis_index("core")
    y, bank = lax.axis_index("chan"), lax.axis_index("bank")
    z = zh * 2 + bank

    owner_chip = plane_index((block_ids >> 2) & 3, (block_ids >> 4) * 2 + (block_ids & 1))
    owner_core = (block_ids >> 1) & 1
    my_chip = plane_index(x, z)
    halves = templates.reshape(NY, 2, NX, 4, 2, SUB, TLEN).transpose(1, 3, 2, 4, 0, 5, 6)
    halves = halves.reshape(2, 32, NY * SUB, TLEN)
    given = lax.dynamic_index_in_dim(halves, 1 - core, 0, keepdims=False)
    received = shift(given, "core", 1)
    mine = lax.dynamic_index_in_dim(halves, core, 0, keepdims=False)

    leading = record[:, :HALO]
    following = lax.ppermute(leading, BLOCKS, [(i, i - 1) for i in range(1, 64)])

    extended = jnp.concatenate([record, following], 1)
    delayed = jnp.zeros((128, EXT), jnp.bfloat16)
    for group_id in range(GROUPS):
        moved = extended[:, DSTEP * group_id : DSTEP * group_id + EXT]
        delayed = jnp.where((sensor_group == group_id)[:, None], moved, delayed)
    first_core = jnp.where(owner_chip[0] == my_chip, owner_core[0], owner_core[1])
    block = jnp.where(first_core == core, mine, received)
    delayed, block = lax.optimization_barrier((delayed, block))
    sensors = [delayed] + [shift(delayed, "chan", d) for d in (1, 2, 3)]
    x2, energy = spread(sensors)
    got = lax.all_to_all(block, PLANE, 0, 0, tiled=True)
    clash = (owner_chip[0] == owner_chip[1]) & (owner_core[0] != owner_core[1])

    def second():
        block = jnp.where(owner_core[1] == core, mine, received)
        return lax.all_to_all(block, PLANE, 0, 0, tiled=True)[owner_chip[1]]

    spare = lax.cond(clash, second, lambda: jnp.zeros(mine.shape[1:], mine.dtype))
    piece = jnp.stack([got[owner_chip[0]], jnp.where(clash, spare, got[owner_chip[1]])])

    piece, x2, energy = lax.optimization_barrier((piece, x2, energy))
    piece = piece.reshape(2, NY, SUB, TLEN)
    parts = [lax.dynamic_index_in_dim(piece, y, 1, keepdims=False)]
    for d in (1, 2, 3):
        part = lax.dynamic_index_in_dim(piece, (y + d) % NY, 1, keepdims=False)
        parts.append(shift(part, "chan", d))
    piece = turn(parts)

    column = join(x, [piece] + [shift(piece, "x", d) for d in (1, 2, 3)])
    column, x2, energy = lax.optimization_barrier((column, x2, energy))
    offsets = jnp.array([0, 1, -1, 2, -2, 3, -3, 4], jnp.int32)
    index = jnp.concatenate([(z - offsets) % NZ, core[None]]).astype(jnp.int32)
    arrived, ahead, behind, sums = [column], column, column, None
    for i in range(4):
        if i < 3:
            nearer, farther = shift(ahead, ZAXES, 1), shift(behind, ZAXES, -1)
        else:
            nearer = shift(ahead[: HALF // 2], ZAXES, 1)
            farther = shift(behind[HALF // 2 :], ZAXES, -1)
        lefts = [[block, shift(block, "core", 1)] for block in arrived]
        places = range(max(0, 2 * i - 1), 2 * i + 1)
        sums = correlate(index, places, lefts, x2, sums)
        ahead, behind, sums = lax.optimization_barrier((nearer, farther, sums))
        arrived = [ahead, behind]
    lefts = [[ahead, behind, shift(ahead, "core", 1), shift(behind, "core", 1)]]
    return correlate(index, [7], lefts, x2, sums, energy)


def solution(mesh):
    fine = Mesh(mesh.devices.reshape(4, NX, 2, NY, 2), ("zh", "x", "core", "chan", "bank"))
    return jax.shard_map(
        local,
        mesh=fine,
        in_specs=(P("chan", BLOCKS), P(BLOCKS, "chan", None), P(), P("chan")),
        out_specs=P(None, "chan", BLOCKS),
        check_vma=False,
    )
```

```python
import math

import jax
import jax.numpy as jnp
from jax import lax
from jax.experimental import pallas as pl
from jax.experimental.pallas import tpu as pltpu
from jax.sharding import Mesh, PartitionSpec as P

SENSORS = 512
TLEN = 256
GROUPS = 4
DSTEP = 64
HALO = 512
TILE = 2048
EXT = TILE + TLEN
FINE = 8
COARSE = TLEN // FINE
NX, NZ, NY = 4, 8, 4
SUB = 16
DEPTH = FINE * NY * SUB
ROWS = 2 * COARSE
HALF = NX * ROWS
TIME_TILE = 768
VMEM_LIMIT = 12 * 1024 * 1024

PLANE = ("zh", "x", "bank")
ZAXES = ("zh", "bank")
BLOCKS = ("zh", "x", "core", "bank")


def shift(value, axis, steps):
    count = lax.axis_size(axis)
    return lax.ppermute(value, axis, [(i, (i + steps) % count) for i in range(count)])


def plane_index(x, z):
    return ((z // 2) * NX + x) * 2 + z % 2


def turn_kernel(*refs):
    inputs, out_ref, turned_ref = refs[:NY], refs[NY], refs[NY + 1]
    rows = [ref[r].astype(jnp.float32) for r in range(2) for ref in inputs]
    turned_ref[...] = jnp.concatenate(rows, 0).T
    for pair in range(FINE // 2):
        even = turned_ref[pl.ds(2 * pair, COARSE, stride=FINE), :].astype(jnp.bfloat16)
        odd = turned_ref[pl.ds(2 * pair + 1, COARSE, stride=FINE), :].astype(jnp.bfloat16)
        for r in range(2):
            lanes = slice(64 * r, 64 * r + 64)
            out_ref[COARSE * r : COARSE * (r + 1), 128 * pair : 128 * (pair + 1)] = jnp.concatenate(
                [even[:, lanes], odd[:, lanes]], 1
            )


def turn(parts):
    return pl.pallas_call(
        turn_kernel,
        out_shape=jax.ShapeDtypeStruct((ROWS, DEPTH), jnp.bfloat16),
        scratch_shapes=[pltpu.VMEM((TLEN, 128), jnp.float32)],
        compiler_params=pltpu.CompilerParams(vmem_limit_bytes=VMEM_LIMIT),
        name="turn",
    )(*parts)


def join_kernel(x_ref, *refs):
    inputs, out_ref, wide_ref = refs[:NX], refs[NX], refs[NX + 1]
    for d, ref in enumerate(inputs):
        kk = lax.rem(x_ref[0] + NX - d, NX)
        for r in range(2):
            block = ref[COARSE * r : COARSE * (r + 1), :].astype(jnp.float32)
            for i in range(DEPTH // 128):
                rows = pl.ds(NX * r + kk, COARSE, stride=2 * NX)
                wide_ref[i, rows, :] = block[:, 128 * i : 128 * (i + 1)]
    for i in range(DEPTH // 128):
        out_ref[:, 128 * i : 128 * (i + 1)] = wide_ref[i].astype(jnp.bfloat16)


def join(x, parts):
    return pl.pallas_call(
        join_kernel,
        grid_spec=pltpu.PrefetchScalarGridSpec(
            num_scalar_prefetch=1,
            grid=(1,),
            in_specs=[pl.BlockSpec((ROWS, DEPTH), lambda n, i: (0, 0))] * NX,
            out_specs=pl.BlockSpec((HALF, DEPTH), lambda n, i: (0, 0)),
            scratch_shapes=[pltpu.VMEM((DEPTH // 128, HALF, 128), jnp.float32)],
        ),
        out_shape=jax.ShapeDtypeStruct((HALF, DEPTH), jnp.bfloat16),
        compiler_params=pltpu.CompilerParams(vmem_limit_bytes=VMEM_LIMIT),
        name="join",
    )(x[None], *parts)


def spread_kernel(*refs):
    near, low, high, x2_ref, energy_ref = refs[:3], refs[3], refs[4], refs[5], refs[6]

    def section(sub, power, far, base):
        rows = pl.ds(pl.multiple_of(sub * SUB, SUB), SUB)
        far_rows = pl.ds(pl.multiple_of((sub - base) * SUB, SUB), SUB)
        blocks = [near[0][rows, :], near[1][rows, :], far[far_rows, :], near[2][rows, :]]
        block = jnp.concatenate([part.astype(jnp.float32) for part in blocks], 0)
        for e in range(FINE):
            moved = pltpu.roll(block, EXT - e, 1) if e else block
            x2_ref[sub, 64 * e : 64 * (e + 1), :] = moved.astype(jnp.bfloat16)
        return power + jnp.sum((block * block).reshape(NY * SUB // 8, 8, EXT), 0)

    total = jnp.zeros((8, EXT), jnp.float32)
    total = lax.fori_loop(0, NZ // 2, lambda i, c: section(i, c, low, 0), total)
    total = lax.fori_loop(NZ // 2, NZ, lambda i, c: section(i, c, high, NZ // 2), total)
    width = 1
    while width < TLEN:
        total = total + pltpu.roll(total, EXT - width, 1)
        width *= 2
    energy_ref[...] = jnp.sum(total, 0, keepdims=True)[:, :TILE]


def spread(sensors):
    return pl.pallas_call(
        spread_kernel,
        out_shape=[
            pltpu.VMEM((NZ, DEPTH, EXT), jnp.bfloat16),
            jax.ShapeDtypeStruct((1, TILE), jnp.float32),
        ],
        compiler_params=pltpu.CompilerParams(vmem_limit_bytes=VMEM_LIMIT),
        cost_estimate=pl.CostEstimate(flops=2**24, bytes_accessed=24 * 2**20, transcendentals=0),
        name="spread",
    )(*sensors)


def square_sums(refs):
    total = None
    for ref in refs:
        wide = ref[...].astype(jnp.float32)
        wide = wide * wide
        for i in range(0, DEPTH, 128):
            part = wide[:, i : i + 128]
            total = part if total is None else total + part
    return jnp.sum(total.reshape(COARSE, 8, 128), 0)


def fold(y_ref, half):
    split = COARSE // 2
    parts = []
    for j in range(split):
        near, far = 8 * j, 8 * (j + split)
        parts.append(y_ref[half, near : near + 8, : EXT - 128] + y_ref[half, far : far + 8, 128:])
    width = FINE
    while len(parts) > 1:
        parts = [
            parts[i] + pltpu.roll(parts[i + 1], EXT - 128 - width, 1)
            for i in range(0, len(parts), 2)
        ]
        width *= 2
    return parts[0][:, :TILE]


def correlate_kernel(count, places, seeded, closing, index_ref, *refs):
    refs = list(refs)
    take = lambda n: [refs.pop(0) for _ in range(n)]
    lefts = [take(count), take(count)]
    x2_ref = take(1)[0]
    before = take(2) if seeded else None
    energy_ref = take(1)[0] if closing else None
    outs = take(1 if closing else 2)
    y_ref = take(1)[0]
    sums, norms = [], []
    for half in range(2):
        for t in range(0, EXT, TIME_TILE):
            total = None
            for ref, place in zip(lefts[half], places):
                right = x2_ref[index_ref[place], :, t : t + TIME_TILE]
                term = jnp.dot(ref[...], right, preferred_element_type=jnp.float32)
                total = term if total is None else total + term
            y_ref[half, :, t : t + TIME_TILE] = total
        rows = slice(8 * half, 8 * half + 8)
        sums.append(fold(y_ref, half))
        norms.append(square_sums(lefts[half]))
        if seeded:
            sums[half] = sums[half] + before[0][rows, :]
            norms[half] = norms[half] + before[1][rows, :]
        if not closing:
            outs[0][rows, :] = sums[half]
            outs[1][rows, :] = norms[half]
    if not closing:
        return
    scale = math.sqrt(SENSORS * TLEN)
    level = energy_ref[...] + 1e-05
    for half in range(2):
        squares = jnp.sum(norms[half], 1, keepdims=True)
        sums[half] = sums[half] * scale * lax.rsqrt(squares * level)
    first = index_ref[NZ] == 0
    low = jnp.where(first, sums[0], sums[1])
    high = jnp.where(first, sums[1], sums[0])
    for r in range(2):
        outs[0][r, :NX, :] = low[NX * r : NX * (r + 1)]
        outs[0][r, NX:, :] = high[NX * r : NX * (r + 1)]


def correlate(index, places, own, other, x2, before=None, energy=None):
    count = len(own)
    seeded, closing = before is not None, energy is not None
    extra = (list(before) if seeded else []) + ([energy] if closing else [])
    operands = [*own, *other, x2, *extra]
    if closing:
        out_shape = jax.ShapeDtypeStruct((2, 8, TILE), jnp.float32)
    else:
        out_shape = [
            jax.ShapeDtypeStruct((16, TILE), jnp.float32),
            jax.ShapeDtypeStruct((16, 128), jnp.float32),
        ]
    return pl.pallas_call(
        lambda *refs: correlate_kernel(count, list(places), seeded, closing, *refs),
        in_specs=[pl.BlockSpec(memory_space=pltpu.SMEM)]
        + [pl.BlockSpec(memory_space=pltpu.VMEM)] * len(operands),
        scratch_shapes=[pltpu.VMEM((2, HALF, EXT), jnp.float32)],
        out_shape=out_shape,
        compiler_params=pltpu.CompilerParams(vmem_limit_bytes=VMEM_LIMIT),
        cost_estimate=pl.CostEstimate(
            flops=2 * 2 * HALF * DEPTH * count * EXT,
            bytes_accessed=count * 3 * 2**20,
            transcendentals=0,
        ),
        name="correlate",
    )(index, *operands)


def local(record, templates, block_ids, sensor_group):
    zh, x, core = lax.axis_index("zh"), lax.axis_index("x"), lax.axis_index("core")
    y, bank = lax.axis_index("chan"), lax.axis_index("bank")
    z = zh * 2 + bank

    owner_chip = plane_index((block_ids >> 2) & 3, (block_ids >> 4) * 2 + (block_ids & 1))
    owner_core = (block_ids >> 1) & 1
    my_chip = plane_index(x, z)
    halves = templates.reshape(NY, 2, NX, 4, 2, SUB, TLEN).transpose(1, 3, 2, 4, 0, 5, 6)
    halves = halves.reshape(2, 32, NY * SUB, TLEN)
    given = lax.dynamic_index_in_dim(halves, 1 - core, 0, keepdims=False)
    received = shift(given, "core", 1)
    mine = lax.dynamic_index_in_dim(halves, core, 0, keepdims=False)

    leading = record[:, :HALO]
    following = lax.ppermute(leading, BLOCKS, [(i, i - 1) for i in range(1, 64)])

    extended = jnp.concatenate([record, following], 1)
    delayed = jnp.zeros((128, EXT), jnp.bfloat16)
    for group_id in range(GROUPS):
        moved = extended[:, DSTEP * group_id : DSTEP * group_id + EXT]
        delayed = jnp.where((sensor_group == group_id)[:, None], moved, delayed)
    first_core = jnp.where(owner_chip[0] == my_chip, owner_core[0], owner_core[1])
    block = jnp.where(first_core == core, mine, received)
    delayed, block = lax.optimization_barrier((delayed, block))
    above, below = shift(delayed, "chan", 1), shift(delayed, "chan", -1)
    above, below = lax.optimization_barrier((above, below))
    low, high = shift(above[:64], "chan", 1), shift(below[64:], "chan", -1)
    got = lax.all_to_all(block, PLANE, 0, 0, tiled=True)
    clash = (owner_chip[0] == owner_chip[1]) & (owner_core[0] != owner_core[1])

    def second():
        block = jnp.where(owner_core[1] == core, mine, received)
        return lax.all_to_all(block, PLANE, 0, 0, tiled=True)[owner_chip[1]]

    spare = lax.cond(clash, second, lambda: jnp.zeros(mine.shape[1:], mine.dtype))
    piece = jnp.stack([got[owner_chip[0]], jnp.where(clash, spare, got[owner_chip[1]])])

    piece, low, high = lax.optimization_barrier((piece, low, high))
    x2, energy = spread([delayed, above, below, low, high])
    piece = piece.reshape(2, NY, SUB, TLEN)
    parts = [lax.dynamic_index_in_dim(piece, y, 1, keepdims=False)]
    for d in (1, 2, 3):
        part = lax.dynamic_index_in_dim(piece, (y + d) % NY, 1, keepdims=False)
        parts.append(shift(part, "chan", d))
    parts, x2, energy = lax.optimization_barrier((parts, x2, energy))
    piece = turn(parts)

    column = join(x, [piece] + [shift(piece, "x", d) for d in (1, 2, 3)])
    offsets = jnp.array([0, 1, -1, 2, -2, 3, -3, 4], jnp.int32)
    index = jnp.concatenate([(z - offsets) % NZ, core[None]]).astype(jnp.int32)
    arrived, ahead, behind, sums = [column], column, column, None
    for i in range(4):
        if i < 3:
            nearer, farther = shift(ahead, ZAXES, 1), shift(behind, ZAXES, -1)
        else:
            nearer = shift(ahead[: HALF // 2], ZAXES, 1)
            farther = shift(behind[HALF // 2 :], ZAXES, -1)
        other = [shift(block, "core", 1) for block in arrived]
        places = range(max(0, 2 * i - 1), 2 * i + 1)
        sums = correlate(index, places, arrived, other, x2, sums)
        ahead, behind, sums = lax.optimization_barrier((nearer, farther, sums))
        arrived = [ahead, behind]
    last = jnp.concatenate([ahead, behind], 0)
    return correlate(index, [7], [last], [shift(last, "core", 1)], x2, sums, energy)


def solution(mesh):
    fine = Mesh(mesh.devices.reshape(4, NX, 2, NY, 2), ("zh", "x", "core", "chan", "bank"))
    return jax.shard_map(
        local,
        mesh=fine,
        in_specs=(P("chan", BLOCKS), P(BLOCKS, "chan", None), P(), P("chan")),
        out_specs=P(None, "chan", BLOCKS),
        check_vma=False,
    )
```

```python
import math

import jax
import jax.numpy as jnp
from jax import lax
from jax.experimental import pallas as pl
from jax.experimental.pallas import tpu as pltpu
from jax.sharding import Mesh, PartitionSpec as P

SENSORS = 512
TLEN = 256
GROUPS = 4
DSTEP = 64
HALO = 512
TILE = 2048
EXT = TILE + TLEN
FINE = 8
COARSE = TLEN // FINE
NX, NZ, NY = 4, 8, 4
SUB = 16
DEPTH = FINE * NY * SUB
ROWS = 2 * COARSE
HALF = NX * ROWS
TIME_TILE = 768
VMEM_LIMIT = 12 * 1024 * 1024

PLANE = ("x", "zh", "bank")
ZAXES = ("zh", "bank")
BLOCKS = ("zh", "x", "core", "bank")


def shift(value, axis, steps):
    count = lax.axis_size(axis)
    return lax.ppermute(value, axis, [(i, (i + steps) % count) for i in range(count)])


def plane_index(x, z):
    return x * NZ + z


def owner_place(ids_ref, r):
    block = ids_ref[r]
    chip = plane_index((block >> 2) & 3, (block >> 4) * 2 + (block & 1))
    return chip, (block >> 1) & 1


def plan_kernel(ids_ref, out_ref):
    places = [owner_place(ids_ref, r) for r in range(2)]
    clash = jnp.logical_and(places[0][0] == places[1][0], places[0][1] != places[1][1])
    out_ref[0] = clash.astype(jnp.int32)
    out_ref[1] = places[0][0]
    out_ref[2] = places[1][0]
    out_ref[3] = places[0][1]
    out_ref[4] = places[1][1]


def plan(block_ids):
    return pl.pallas_call(
        plan_kernel,
        in_specs=[pl.BlockSpec(memory_space=pltpu.SMEM)],
        out_specs=pl.BlockSpec(memory_space=pltpu.SMEM),
        out_shape=jax.ShapeDtypeStruct((5,), jnp.int32),
        compiler_params=pltpu.CompilerParams(vmem_limit_bytes=VMEM_LIMIT),
        name="plan",
    )(block_ids)


def turn_kernel(*refs):
    inputs, out_ref, turned_ref = refs[:NY], refs[NY], refs[NY + 1]
    rows = [ref[r].astype(jnp.float32) for r in range(2) for ref in inputs]
    turned_ref[...] = jnp.concatenate(rows, 0).T
    for pair in range(FINE // 2):
        even = turned_ref[pl.ds(2 * pair, COARSE, stride=FINE), :].astype(jnp.bfloat16)
        odd = turned_ref[pl.ds(2 * pair + 1, COARSE, stride=FINE), :].astype(jnp.bfloat16)
        for r in range(2):
            lanes = slice(64 * r, 64 * r + 64)
            out_ref[COARSE * r : COARSE * (r + 1), 128 * pair : 128 * (pair + 1)] = jnp.concatenate(
                [even[:, lanes], odd[:, lanes]], 1
            )


def turn(parts):
    return pl.pallas_call(
        turn_kernel,
        out_shape=jax.ShapeDtypeStruct((ROWS, DEPTH), jnp.bfloat16),
        scratch_shapes=[pltpu.VMEM((TLEN, 128), jnp.float32)],
        compiler_params=pltpu.CompilerParams(vmem_limit_bytes=VMEM_LIMIT),
        name="turn",
    )(*parts)


def join_kernel(x_ref, *refs):
    inputs, out_ref, wide_ref = refs[:NX], refs[NX], refs[NX + 1]
    for d, ref in enumerate(inputs):
        kk = lax.rem(x_ref[0] + NX - d, NX)
        for r in range(2):
            block = ref[COARSE * r : COARSE * (r + 1), :].astype(jnp.float32)
            for i in range(DEPTH // 128):
                rows = pl.ds(NX * r + kk, COARSE, stride=2 * NX)
                wide_ref[i, rows, :] = block[:, 128 * i : 128 * (i + 1)]
    for i in range(DEPTH // 128):
        out_ref[:, 128 * i : 128 * (i + 1)] = wide_ref[i].astype(jnp.bfloat16)


def join(x, parts):
    return pl.pallas_call(
        join_kernel,
        grid_spec=pltpu.PrefetchScalarGridSpec(
            num_scalar_prefetch=1,
            grid=(1,),
            in_specs=[pl.BlockSpec((ROWS, DEPTH), lambda n, i: (0, 0))] * NX,
            out_specs=pl.BlockSpec((HALF, DEPTH), lambda n, i: (0, 0)),
            scratch_shapes=[pltpu.VMEM((DEPTH // 128, HALF, 128), jnp.float32)],
        ),
        out_shape=jax.ShapeDtypeStruct((HALF, DEPTH), jnp.bfloat16),
        compiler_params=pltpu.CompilerParams(vmem_limit_bytes=VMEM_LIMIT),
        name="join",
    )(x[None], *parts)


def spread_kernel(base, sources, power, x2_ref):
    def section(sub, power):
        rows = pl.ds(pl.multiple_of((sub - base) * SUB, SUB), SUB)
        block = jnp.concatenate([ref[rows, :].astype(jnp.float32) for ref in sources], 0)
        for e in range(FINE):
            moved = pltpu.roll(block, EXT - e, 1) if e else block
            x2_ref[sub, 64 * e : 64 * (e + 1), :] = moved.astype(jnp.bfloat16)
        return power + jnp.sum((block * block).reshape(NY * SUB // 8, 8, EXT), 0)

    return lax.fori_loop(base, base + NZ // 2, section, power)


def spread_low_kernel(*refs):
    sources, x2_ref, power_ref = refs[:NY], refs[NY], refs[NY + 1]
    power_ref[...] = spread_kernel(0, sources, jnp.zeros((8, EXT), jnp.float32), x2_ref)


def spread_high_kernel(*refs):
    sources, before_ref, x2_ref, energy_ref = refs[:NY], refs[NY], refs[NY + 2], refs[NY + 3]
    total = spread_kernel(NZ // 2, sources, before_ref[...], x2_ref)
    width = 1
    while width < TLEN:
        total = total + pltpu.roll(total, EXT - width, 1)
        width *= 2
    energy_ref[...] = jnp.sum(total, 0, keepdims=True)[:, :TILE]


def spread(sources, before=None):
    x2 = pltpu.VMEM((NZ, DEPTH, EXT), jnp.bfloat16)
    power, energy = (8, EXT), (1, TILE)
    return pl.pallas_call(
        spread_high_kernel if before else spread_low_kernel,
        in_specs=[pl.BlockSpec(memory_space=pltpu.VMEM)] * (NY + 2 if before else NY),
        out_shape=[x2, jax.ShapeDtypeStruct(energy if before else power, jnp.float32)],
        input_output_aliases={NY + 1: 0} if before else {},
        compiler_params=pltpu.CompilerParams(vmem_limit_bytes=VMEM_LIMIT),
        cost_estimate=pl.CostEstimate(flops=2**23, bytes_accessed=12 * 2**20, transcendentals=0),
        name="spread",
    )(*sources, *(before or ()))


def square_sums(refs):
    total = None
    for ref in refs:
        wide = ref[...].astype(jnp.float32)
        wide = wide * wide
        for i in range(0, DEPTH, 128):
            part = wide[:, i : i + 128]
            total = part if total is None else total + part
    return jnp.sum(total.reshape(COARSE, 8, 128), 0)


def fold(y_ref, half):
    split = COARSE // 2
    parts = []
    for j in range(split):
        near, far = 8 * j, 8 * (j + split)
        parts.append(y_ref[half, near : near + 8, : EXT - 128] + y_ref[half, far : far + 8, 128:])
    width = FINE
    while len(parts) > 1:
        parts = [
            parts[i] + pltpu.roll(parts[i + 1], EXT - 128 - width, 1)
            for i in range(0, len(parts), 2)
        ]
        width *= 2
    return parts[0][:, :TILE]


def correlate_kernel(count, places, seeded, closing, index_ref, *refs):
    refs = list(refs)
    take = lambda n: [refs.pop(0) for _ in range(n)]
    lefts = [take(count), take(count)]
    x2_ref = take(1)[0]
    before = take(2) if seeded else None
    energy_ref = take(1)[0] if closing else None
    outs = take(1 if closing else 2)
    y_ref = take(1)[0]
    sums, norms = [], []
    for half in range(2):
        for t in range(0, EXT, TIME_TILE):
            total = None
            for ref, place in zip(lefts[half], places):
                right = x2_ref[index_ref[place], :, t : t + TIME_TILE]
                term = jnp.dot(ref[...], right, preferred_element_type=jnp.float32)
                total = term if total is None else total + term
            y_ref[half, :, t : t + TIME_TILE] = total
        rows = slice(8 * half, 8 * half + 8)
        sums.append(fold(y_ref, half))
        norms.append(square_sums(lefts[half]))
        if seeded:
            sums[half] = sums[half] + before[0][rows, :]
            norms[half] = norms[half] + before[1][rows, :]
        if not closing:
            outs[0][rows, :] = sums[half]
            outs[1][rows, :] = norms[half]
    if not closing:
        return
    scale = math.sqrt(SENSORS * TLEN)
    level = energy_ref[...] + 1e-05
    for half in range(2):
        squares = jnp.sum(norms[half], 1, keepdims=True)
        sums[half] = sums[half] * scale * lax.rsqrt(squares * level)
    first = index_ref[NZ] == 0
    low = jnp.where(first, sums[0], sums[1])
    high = jnp.where(first, sums[1], sums[0])
    for r in range(2):
        outs[0][r, :NX, :] = low[NX * r : NX * (r + 1)]
        outs[0][r, NX:, :] = high[NX * r : NX * (r + 1)]


def correlate(index, places, own, other, x2, before=None, energy=None):
    count = len(own)
    seeded, closing = before is not None, energy is not None
    extra = (list(before) if seeded else []) + ([energy] if closing else [])
    operands = [*own, *other, x2, *extra]
    if closing:
        out_shape = jax.ShapeDtypeStruct((2, 8, TILE), jnp.float32)
    else:
        out_shape = [
            jax.ShapeDtypeStruct((16, TILE), jnp.float32),
            jax.ShapeDtypeStruct((16, 128), jnp.float32),
        ]
    return pl.pallas_call(
        lambda *refs: correlate_kernel(count, list(places), seeded, closing, *refs),
        in_specs=[pl.BlockSpec(memory_space=pltpu.SMEM)]
        + [pl.BlockSpec(memory_space=pltpu.VMEM)] * len(operands),
        scratch_shapes=[pltpu.VMEM((2, HALF, EXT), jnp.float32)],
        out_shape=out_shape,
        compiler_params=pltpu.CompilerParams(vmem_limit_bytes=VMEM_LIMIT),
        cost_estimate=pl.CostEstimate(
            flops=2 * 2 * HALF * DEPTH * count * EXT,
            bytes_accessed=count * 3 * 2**20,
            transcendentals=0,
        ),
        name="correlate",
    )(index, *operands)


def local(record, templates, block_ids, sensor_group):
    zh, x, core = lax.axis_index("zh"), lax.axis_index("x"), lax.axis_index("core")
    y, bank = lax.axis_index("chan"), lax.axis_index("bank")
    z = zh * 2 + bank

    places = plan(block_ids)
    clash, chip0, chip1, core0, core1 = [places[i] for i in range(5)]
    owner_chip, owner_core, clash = (chip0, chip1), (core0, core1), clash != 0
    my_chip = plane_index(x, z)
    halves = templates.reshape(NY, 2, NX, NZ, SUB, TLEN).transpose(1, 2, 3, 0, 4, 5)
    halves = halves.reshape(2, 32, NY * SUB, TLEN)
    given = lax.dynamic_index_in_dim(halves, 1 - core, 0, keepdims=False)
    received = shift(given, "core", 1)
    mine = lax.dynamic_index_in_dim(halves, core, 0, keepdims=False)

    leading = record[:, :HALO]
    following = lax.ppermute(leading, BLOCKS, [(i, i - 1) for i in range(1, 64)])

    def moveout(rows):
        extended = jnp.concatenate([record[rows], following[rows]], 1)
        group, delayed = sensor_group[rows, None], jnp.zeros((64, EXT), jnp.bfloat16)
        for group_id in range(GROUPS):
            moved = extended[:, DSTEP * group_id : DSTEP * group_id + EXT]
            delayed = jnp.where(group == group_id, moved, delayed)
        return delayed

    low, high = moveout(slice(0, 64)), moveout(slice(64, 128))

    first_core = jnp.where(owner_chip[0] == my_chip, owner_core[0], owner_core[1])
    block = jnp.where(first_core == core, mine, received)
    low, high, block = lax.optimization_barrier((low, high, block))
    low_above, high_below = shift(low, "chan", 1), shift(high, "chan", -1)
    low_below, high_above = shift(low, "chan", -1), shift(high, "chan", 1)
    low_far, high_far = shift(low_above, "chan", 1), shift(high_below, "chan", -1)
    lows, highs = [low, low_above, low_far, low_below], [high, high_above, high_far, high_below]
    got = lax.all_to_all(block, PLANE, 0, 0, tiled=True)

    def second():
        block = jnp.where(owner_core[1] == core, mine, received)
        return lax.all_to_all(block, PLANE, 0, 0, tiled=True)[owner_chip[1]]

    spare = lax.cond(clash, second, lambda: jnp.zeros(mine.shape[1:], mine.dtype))
    piece = jnp.stack([got[owner_chip[0]], jnp.where(clash, spare, got[owner_chip[1]])])

    piece, lows, highs = lax.optimization_barrier((piece, lows, highs))
    x2, power = spread(lows)
    piece = piece.reshape(2, NY, SUB, TLEN)
    parts = [lax.dynamic_index_in_dim(piece, y, 1, keepdims=False)]
    for d in (1, 2, 3):
        part = lax.dynamic_index_in_dim(piece, (y + d) % NY, 1, keepdims=False)
        parts.append(shift(part, "chan", d))
    parts, x2, power = lax.optimization_barrier((parts, x2, power))
    piece = turn(parts)

    x2, energy = spread(highs, (power, x2))
    pieces = [piece] + [shift(piece, "x", d) for d in (1, 2, 3)]
    pieces, x2, energy = lax.optimization_barrier((pieces, x2, energy))
    column = join(x, pieces)
    offsets = jnp.array([0, 1, -1, 2, -2, 3, -3, 4], jnp.int32)
    index = jnp.concatenate([(z - offsets) % NZ, core[None]]).astype(jnp.int32)
    arrived, ahead, behind, sums = [column], column, column, None
    for i in range(4):
        nearer = shift(ahead, ZAXES, 1)
        farther = shift(behind, ZAXES, -1) if i < 3 else behind
        other = [shift(block, "core", 1) for block in arrived]
        places = range(max(0, 2 * i - 1), 2 * i + 1)
        sums = correlate(index, places, arrived, other, x2, sums)
        ahead, behind, sums = lax.optimization_barrier((nearer, farther, sums))
        arrived = [ahead, behind]
    return correlate(index, [7], [ahead], [shift(ahead, "core", 1)], x2, sums, energy)


def solution(mesh):
    fine = Mesh(mesh.devices.reshape(4, NX, 2, NY, 2), ("zh", "x", "core", "chan", "bank"))
    return jax.shard_map(
        local,
        mesh=fine,
        in_specs=(P("chan", BLOCKS), P(BLOCKS, "chan", None), P(), P("chan")),
        out_specs=P(None, "chan", BLOCKS),
        check_vma=False,
    )
```

```python
import math

import jax
import jax.numpy as jnp
from jax import lax
from jax.experimental import pallas as pl
from jax.experimental.pallas import tpu as pltpu
from jax.sharding import Mesh, PartitionSpec as P

SENSORS = 512
TLEN = 256
GROUPS = 4
DSTEP = 64
HALO = 512
TILE = 2048
EXT = TILE + TLEN
FINE = 8
COARSE = TLEN // FINE
NX, NZ, NY = 4, 8, 4
SUB = 16
DEPTH = FINE * NY * SUB
ROWS = 2 * COARSE
HALF = NX * ROWS
TIME_TILE = 768
VMEM_LIMIT = 12 * 1024 * 1024

PLANE = ("x", "zh", "bank")
ZAXES = ("zh", "bank")
BLOCKS = ("zh", "x", "core", "bank")


def shift(value, axis, steps):
    count = lax.axis_size(axis)
    return lax.ppermute(value, axis, [(i, (i + steps) % count) for i in range(count)])


def round_z(value, way):
    place = lambda z, core: z % NZ // 2 * 4 + core * 2 + z % 2
    pairs = []
    for z in range(NZ):
        pairs += [(place(z, 0), place(z + way, 0)), (place(z, 1), place(z - way, 1))]
    return lax.ppermute(value, ("zh", "core", "bank"), pairs)


def plane_index(x, z):
    return x * NZ + z


def owner_place(ids_ref, r):
    block = ids_ref[r]
    chip = plane_index((block >> 2) & 3, (block >> 4) * 2 + (block & 1))
    return chip, (block >> 1) & 1


def plan_kernel(ids_ref, out_ref):
    places = [owner_place(ids_ref, r) for r in range(2)]
    clash = jnp.logical_and(places[0][0] == places[1][0], places[0][1] != places[1][1])
    out_ref[0] = clash.astype(jnp.int32)
    out_ref[1] = places[0][0]
    out_ref[2] = places[1][0]
    out_ref[3] = places[0][1]
    out_ref[4] = places[1][1]


def plan(block_ids):
    return pl.pallas_call(
        plan_kernel,
        in_specs=[pl.BlockSpec(memory_space=pltpu.SMEM)],
        out_specs=pl.BlockSpec(memory_space=pltpu.SMEM),
        out_shape=jax.ShapeDtypeStruct((5,), jnp.int32),
        compiler_params=pltpu.CompilerParams(vmem_limit_bytes=VMEM_LIMIT),
        name="plan",
    )(block_ids)


def turn_kernel(*refs):
    inputs, out_ref, turned_ref = refs[:NY], refs[NY], refs[NY + 1]
    rows = [ref[r].astype(jnp.float32) for r in range(2) for ref in inputs]
    turned_ref[...] = jnp.concatenate(rows, 0).T
    for pair in range(FINE // 2):
        even = turned_ref[pl.ds(2 * pair, COARSE, stride=FINE), :].astype(jnp.bfloat16)
        odd = turned_ref[pl.ds(2 * pair + 1, COARSE, stride=FINE), :].astype(jnp.bfloat16)
        for r in range(2):
            lanes = slice(64 * r, 64 * r + 64)
            out_ref[COARSE * r : COARSE * (r + 1), 128 * pair : 128 * (pair + 1)] = jnp.concatenate(
                [even[:, lanes], odd[:, lanes]], 1
            )


def turn(parts):
    return pl.pallas_call(
        turn_kernel,
        out_shape=jax.ShapeDtypeStruct((ROWS, DEPTH), jnp.bfloat16),
        scratch_shapes=[pltpu.VMEM((TLEN, 128), jnp.float32)],
        compiler_params=pltpu.CompilerParams(vmem_limit_bytes=VMEM_LIMIT),
        name="turn",
    )(*parts)


def join_kernel(x_ref, *refs):
    inputs, out_ref, wide_ref = refs[:NX], refs[NX], refs[NX + 1]
    for d, ref in enumerate(inputs):
        kk = lax.rem(x_ref[0] + NX - d, NX)
        for r in range(2):
            block = ref[COARSE * r : COARSE * (r + 1), :].astype(jnp.float32)
            for i in range(DEPTH // 128):
                rows = pl.ds(NX * r + kk, COARSE, stride=2 * NX)
                wide_ref[i, rows, :] = block[:, 128 * i : 128 * (i + 1)]
    for i in range(DEPTH // 128):
        out_ref[:, 128 * i : 128 * (i + 1)] = wide_ref[i].astype(jnp.bfloat16)


def join(x, parts):
    return pl.pallas_call(
        join_kernel,
        grid_spec=pltpu.PrefetchScalarGridSpec(
            num_scalar_prefetch=1,
            grid=(1,),
            in_specs=[pl.BlockSpec((ROWS, DEPTH), lambda n, i: (0, 0))] * NX,
            out_specs=pl.BlockSpec((HALF, DEPTH), lambda n, i: (0, 0)),
            scratch_shapes=[pltpu.VMEM((DEPTH // 128, HALF, 128), jnp.float32)],
        ),
        out_shape=jax.ShapeDtypeStruct((HALF, DEPTH), jnp.bfloat16),
        compiler_params=pltpu.CompilerParams(vmem_limit_bytes=VMEM_LIMIT),
        name="join",
    )(x[None], *parts)


def spread_kernel(base, sources, power, x2_ref):
    def section(sub, power):
        rows = pl.ds(pl.multiple_of((sub - base) * SUB, SUB), SUB)
        block = jnp.concatenate([ref[rows, :].astype(jnp.float32) for ref in sources], 0)
        for e in range(FINE):
            moved = pltpu.roll(block, EXT - e, 1) if e else block
            x2_ref[sub, 64 * e : 64 * (e + 1), :] = moved.astype(jnp.bfloat16)
        return power + jnp.sum((block * block).reshape(NY * SUB // 8, 8, EXT), 0)

    return lax.fori_loop(base, base + NZ // 2, section, power)


def spread_low_kernel(*refs):
    sources, x2_ref, power_ref = refs[:NY], refs[NY], refs[NY + 1]
    power_ref[...] = spread_kernel(0, sources, jnp.zeros((8, EXT), jnp.float32), x2_ref)


def spread_high_kernel(*refs):
    sources, before_ref, x2_ref, energy_ref = refs[:NY], refs[NY], refs[NY + 2], refs[NY + 3]
    total = spread_kernel(NZ // 2, sources, before_ref[...], x2_ref)
    width = 1
    while width < TLEN:
        total = total + pltpu.roll(total, EXT - width, 1)
        width *= 2
    energy_ref[...] = jnp.sum(total, 0, keepdims=True)[:, :TILE]


def spread(sources, before=None):
    x2 = pltpu.VMEM((NZ, DEPTH, EXT), jnp.bfloat16)
    power, energy = (8, EXT), (1, TILE)
    return pl.pallas_call(
        spread_high_kernel if before else spread_low_kernel,
        in_specs=[pl.BlockSpec(memory_space=pltpu.VMEM)] * (NY + 2 if before else NY),
        out_shape=[x2, jax.ShapeDtypeStruct(energy if before else power, jnp.float32)],
        input_output_aliases={NY + 1: 0} if before else {},
        compiler_params=pltpu.CompilerParams(vmem_limit_bytes=VMEM_LIMIT),
        cost_estimate=pl.CostEstimate(flops=2**23, bytes_accessed=12 * 2**20, transcendentals=0),
        name="spread",
    )(*sources, *(before or ()))


def square_sums(refs):
    total = None
    for ref in refs:
        wide = ref[...].astype(jnp.float32)
        wide = wide * wide
        for i in range(0, DEPTH, 128):
            part = wide[:, i : i + 128]
            total = part if total is None else total + part
    return jnp.sum(total.reshape(COARSE, 8, 128), 0)


def fold(y_ref, half):
    split = COARSE // 2
    parts = []
    for j in range(split):
        near, far = 8 * j, 8 * (j + split)
        parts.append(y_ref[half, near : near + 8, : EXT - 128] + y_ref[half, far : far + 8, 128:])
    width = FINE
    while len(parts) > 1:
        parts = [
            parts[i] + pltpu.roll(parts[i + 1], EXT - 128 - width, 1)
            for i in range(0, len(parts), 2)
        ]
        width *= 2
    return parts[0][:, :TILE]


def chip_row(index_ref, place):
    mirrored = place if place in (0, NZ - 1) else place + (1 if place % 2 else -1)
    return jnp.where(index_ref[NZ] == 0, index_ref[place], index_ref[mirrored])


def correlate_kernel(count, places, seeded, closing, index_ref, *refs):
    refs = list(refs)
    take = lambda n: [refs.pop(0) for _ in range(n)]
    lefts = [take(count), take(count)]
    x2_ref = take(1)[0]
    before = take(2) if seeded else None
    energy_ref = take(1)[0] if closing else None
    outs = take(1 if closing else 2)
    y_ref = take(1)[0]
    sums, norms = [], []
    for half in range(2):
        for t in range(0, EXT, TIME_TILE):
            total = None
            for ref, place in zip(lefts[half], places):
                right = x2_ref[chip_row(index_ref, place), :, t : t + TIME_TILE]
                term = jnp.dot(ref[...], right, preferred_element_type=jnp.float32)
                total = term if total is None else total + term
            y_ref[half, :, t : t + TIME_TILE] = total
        rows = slice(8 * half, 8 * half + 8)
        sums.append(fold(y_ref, half))
        norms.append(square_sums(lefts[half]))
        if seeded:
            sums[half] = sums[half] + before[0][rows, :]
            norms[half] = norms[half] + before[1][rows, :]
        if not closing:
            outs[0][rows, :] = sums[half]
            outs[1][rows, :] = norms[half]
    if not closing:
        return
    scale = math.sqrt(SENSORS * TLEN)
    level = energy_ref[...] + 1e-05
    for half in range(2):
        squares = jnp.sum(norms[half], 1, keepdims=True)
        sums[half] = sums[half] * scale * lax.rsqrt(squares * level)
    first = index_ref[NZ] == 0
    low = jnp.where(first, sums[0], sums[1])
    high = jnp.where(first, sums[1], sums[0])
    for r in range(2):
        outs[0][r, :NX, :] = low[NX * r : NX * (r + 1)]
        outs[0][r, NX:, :] = high[NX * r : NX * (r + 1)]


def correlate(index, places, own, other, x2, before=None, energy=None):
    count = len(own)
    seeded, closing = before is not None, energy is not None
    extra = (list(before) if seeded else []) + ([energy] if closing else [])
    operands = [*own, *other, x2, *extra]
    if closing:
        out_shape = jax.ShapeDtypeStruct((2, 8, TILE), jnp.float32)
    else:
        out_shape = [
            jax.ShapeDtypeStruct((16, TILE), jnp.float32),
            jax.ShapeDtypeStruct((16, 128), jnp.float32),
        ]
    return pl.pallas_call(
        lambda *refs: correlate_kernel(count, list(places), seeded, closing, *refs),
        in_specs=[pl.BlockSpec(memory_space=pltpu.SMEM)]
        + [pl.BlockSpec(memory_space=pltpu.VMEM)] * len(operands),
        scratch_shapes=[pltpu.VMEM((2, HALF, EXT), jnp.float32)],
        out_shape=out_shape,
        compiler_params=pltpu.CompilerParams(vmem_limit_bytes=VMEM_LIMIT),
        cost_estimate=pl.CostEstimate(
            flops=2 * 2 * HALF * DEPTH * count * EXT,
            bytes_accessed=count * 3 * 2**20,
            transcendentals=0,
        ),
        name="correlate",
    )(index, *operands)


def local(record, templates, block_ids, sensor_group):
    zh, x, core = lax.axis_index("zh"), lax.axis_index("x"), lax.axis_index("core")
    y, bank = lax.axis_index("chan"), lax.axis_index("bank")
    z = zh * 2 + bank

    places = plan(block_ids)
    clash, chip0, chip1, core0, core1 = [places[i] for i in range(5)]
    owner_chip, owner_core, clash = (chip0, chip1), (core0, core1), clash != 0
    my_chip = plane_index(x, z)
    halves = templates.reshape(NY, 2, NX, NZ, SUB, TLEN).transpose(1, 2, 3, 0, 4, 5)
    halves = halves.reshape(2, 32, NY * SUB, TLEN)
    given = lax.dynamic_index_in_dim(halves, 1 - core, 0, keepdims=False)
    received = shift(given, "core", 1)
    mine = lax.dynamic_index_in_dim(halves, core, 0, keepdims=False)

    leading = record[:, :HALO]
    following = lax.ppermute(leading, BLOCKS, [(i, i - 1) for i in range(1, 64)])

    def moveout(rows):
        extended = jnp.concatenate([record[rows], following[rows]], 1)
        group, delayed = sensor_group[rows, None], jnp.zeros((64, EXT), jnp.bfloat16)
        for group_id in range(GROUPS):
            moved = extended[:, DSTEP * group_id : DSTEP * group_id + EXT]
            delayed = jnp.where(group == group_id, moved, delayed)
        return delayed

    low, high = moveout(slice(0, 64)), moveout(slice(64, 128))

    first_core = jnp.where(owner_chip[0] == my_chip, owner_core[0], owner_core[1])
    block = jnp.where(first_core == core, mine, received)
    low, high, block = lax.optimization_barrier((low, high, block))
    low_above, high_below = shift(low, "chan", 1), shift(high, "chan", -1)
    low_below, high_above = shift(low, "chan", -1), shift(high, "chan", 1)
    low_far, high_far = shift(low_above, "chan", 1), shift(high_below, "chan", -1)
    lows, highs = [low, low_above, low_far, low_below], [high, high_above, high_far, high_below]
    got = lax.all_to_all(block, PLANE, 0, 0, tiled=True)

    def second():
        block = jnp.where(owner_core[1] == core, mine, received)
        return lax.all_to_all(block, PLANE, 0, 0, tiled=True)[owner_chip[1]]

    spare = lax.cond(clash, second, lambda: jnp.zeros(mine.shape[1:], mine.dtype))
    piece = jnp.stack([got[owner_chip[0]], jnp.where(clash, spare, got[owner_chip[1]])])

    piece, lows, highs = lax.optimization_barrier((piece, lows, highs))
    x2, power = spread(lows)
    piece = piece.reshape(2, NY, SUB, TLEN)
    parts = [lax.dynamic_index_in_dim(piece, y, 1, keepdims=False)]
    for d in (1, 2, 3):
        part = lax.dynamic_index_in_dim(piece, (y + d) % NY, 1, keepdims=False)
        parts.append(shift(part, "chan", d))
    parts, x2, power = lax.optimization_barrier((parts, x2, power))
    piece = turn(parts)

    x2, energy = spread(highs, (power, x2))
    pieces = [piece] + [shift(piece, "x", d) for d in (1, 2, 3)]
    pieces, x2, energy = lax.optimization_barrier((pieces, x2, energy))
    column = join(x, pieces)
    offsets = jnp.array([0, 1, -1, 2, -2, 3, -3, 4], jnp.int32)
    index = jnp.concatenate([(z - offsets) % NZ, core[None]]).astype(jnp.int32)
    arrived, ahead, behind, sums = [column], column, column, None
    for i in range(4):
        nearer = round_z(ahead, 1)
        farther = round_z(behind, -1) if i < 3 else behind
        other = [shift(block, "core", 1) for block in arrived[::-1]]
        places = range(max(0, 2 * i - 1), 2 * i + 1)
        sums = correlate(index, places, arrived, other, x2, sums)
        ahead, behind, sums = lax.optimization_barrier((nearer, farther, sums))
        arrived = [ahead, behind]
    return correlate(index, [7], [ahead], [shift(ahead, "core", 1)], x2, sums, energy)


def solution(mesh):
    fine = Mesh(mesh.devices.reshape(4, NX, 2, NY, 2), ("zh", "x", "core", "chan", "bank"))
    return jax.shard_map(
        local,
        mesh=fine,
        in_specs=(P("chan", BLOCKS), P(BLOCKS, "chan", None), P(), P("chan")),
        out_specs=P(None, "chan", BLOCKS),
        check_vma=False,
    )
```
